32 devices in a mesh: gx: 4 (over z), gy: 4 (over y, x), ta: 2 (over core).
Axes of the slice: x: 2, y: 2, z: 4, core: 2. Of those that a mesh axis runs over, the one named last changes fastest.
Arguments:
- prior_heads: float32 [64, 8, 32, 128], P('ta', 'gx', 'gy')
- facies: int32 [8, 32, 128], P('gx', 'gy'), may hold values from 0 to 5
- facies_cond: float32 [6], replicated, may hold values from 0.1 to 2
- well_cell: int32 [64], P('ta'), may hold values from 0 to 32767, as said below
- pump_rate: float32 [64], P('ta'), may hold values from 1 to 10
- obs_test: int32 [192], P('ta'), may hold values from 0 to 63, as said below
- obs_pair: int32 [192], P('ta'), may hold values from 0 to 63, as said below
Outputs:
- heads: float32 [64, 8, 32, 128], P('ta', 'gx', 'gy')
- jjt: float32 [192, 192], P('ta', ('gx', 'gy'))
The draws below stay inside these ranges and needn't reach their ends.
Inputs may be any that keep to these rules, and one draw needn't show every extreme that they name: `well_cell`: no two tests pump at the same cell. `obs_test`: observation o names a test of group o // 96, that is one of tests (o // 96) * 32 to (o // 96 + 1) * 32 - 1; every test of a group is named by some observation of that group. `obs_pair`: observation o names a test of group o // 96, that is one of tests (o // 96) * 32 to (o // 96 + 1) * 32 - 1; every test of a group is named by some observation of that group.
All inputs are finite; a program needn't handle non-finite values.
Results may differ from the reference program's by a relative error of at most 0.0003.
Values may be sent and summed in bfloat16 or wider, within the bound.
A program may use at most 64 MiB of HBM per device.

```python
import math
import jax
import jax.numpy as jnp
from jax import lax

NZ = 128
R_DEV = 32
OBS_DEV = 96
ITERS = 2
FACIES = 6
NX = 8
NY = 32
TESTS = 64
OBS = 192


def group_tests(key):
    groups = OBS // OBS_DEV
    subkeys = jax.random.split(key, 3)
    covered = jax.vmap(lambda sub_key: jax.random.permutation(sub_key, R_DEV))(jax.random.split(subkeys[0], groups))
    remaining = jax.random.randint(subkeys[1], (groups, OBS_DEV - R_DEV), 0, R_DEV)
    joined = jnp.concatenate([covered.astype(jnp.int32), remaining.astype(jnp.int32)], axis=1)
    shuffle = jax.vmap(lambda sub_key: jax.random.permutation(sub_key, OBS_DEV))(jax.random.split(subkeys[2], groups))
    joined = jnp.take_along_axis(joined, shuffle, axis=1)
    offsets = (jnp.arange(groups, dtype=jnp.int32) * R_DEV)[:, None]
    return (joined + offsets).reshape(OBS).astype(jnp.int32)


def draw_obs_test(key, part):
    return group_tests(jax.random.fold_in(key, 5))


def draw_obs_pair(key, part):
    return group_tests(jax.random.fold_in(key, 7))


def draw_well_cell(key, part):
    return jax.random.permutation(jax.random.fold_in(key, 3), NX * NY * NZ)[:TESTS].astype(jnp.int32)


def draw_prior_heads(key, part):
    subkeys = jax.random.split(jax.random.fold_in(key, 9), 2)
    across_x = (jnp.arange(NX, dtype=jnp.float32) / NX)[:, None, None]
    along_y = (jnp.arange(NY, dtype=jnp.float32) / NY)[None, :, None]
    rising = 1.0 + 0.6 * across_x + 0.6 * along_y
    shared = jax.random.normal(subkeys[0], (NX, NY, NZ), jnp.float32)
    per_test = jax.random.normal(subkeys[1], (TESTS, NX, NY, NZ), jnp.float32)
    return (rising * (shared + 0.7 * per_test)).astype(jnp.float32)


def place_ends(entries, own_key, low, largest):
    spot = [jax.random.randint(jax.random.fold_in(own_key, axis), (), 0, length) for axis, length in enumerate(entries.shape)]
    main_axis = entries.shape.index(max(entries.shape))
    next_to = spot[:main_axis] + [(spot[main_axis] + 1) % entries.shape[main_axis]] + spot[main_axis + 1:]
    return entries.at[tuple(spot)].set(low).at[tuple(next_to)].set(largest)


def steps_of(own_key, dims, cuts, smallest, largest):
    def one(axis_at, shards_of):
        steps = jax.random.uniform(jax.random.fold_in(jax.random.fold_in(own_key, 6), axis_at), (shards_of,), jnp.float32, smallest / len(cuts), largest / len(cuts))
        return jnp.repeat(jnp.exp(steps), dims[axis_at] // shards_of).reshape((-1,) + (1,) * (len(dims) - axis_at - 1))

    gain = one(*cuts[0])
    for cut in cuts[1:]:
        gain = gain * one(*cut)
    return gain


def setup_inputs(seed: int = 0) -> dict:
    key_list = jax.random.split(jax.random.key(seed), 8)
    return {
        "prior_heads": draw_prior_heads(jax.random.fold_in(key_list[7], 71), 0),
        "facies": place_ends(jax.random.randint(key_list[1], (NX, NY, NZ), 0, FACIES), jax.random.fold_in(key_list[1], 1), 0, FACIES - 1).astype(jnp.int32),
        "facies_cond": jnp.clip(jnp.exp(jax.random.uniform(key_list[2], (FACIES,), jnp.float32, math.log(0.1), math.log(2.0))), 0.1, 2.0),
        "well_cell": draw_well_cell(jax.random.fold_in(key_list[7], 71), 0),
        "pump_rate": jnp.clip(jnp.exp(math.log(10.0) - 2.3025851 * jax.random.uniform(key_list[4], (TESTS,), jnp.float32) ** steps_of(key_list[4], (TESTS,), ((0, 2),), -0.2, 0.2)), 1.0, 10.0),
        "obs_test": draw_obs_test(jax.random.fold_in(key_list[7], 71), 0),
        "obs_pair": draw_obs_pair(jax.random.fold_in(key_list[7], 71), 0),
    }


STORAGE = 0.25
HIGHEST_PRECISION = lax.Precision.HIGHEST

def flat_rows(array_in):
    return array_in.reshape(array_in.shape[0], -1)

def gram_local(first_field, second_field):
    return jnp.dot(flat_rows(first_field), flat_rows(second_field).T, precision=HIGHEST_PRECISION)

def combine(coefficients, field_in):
    mixed_rows = jnp.dot(coefficients.T, flat_rows(field_in), precision=HIGHEST_PRECISION)
    return mixed_rows.reshape(field_in.shape)

def solve_spd(matrix, right_side):
    factor = jnp.linalg.cholesky(matrix)
    return jax.scipy.linalg.cho_solve((factor, True), right_side)

def neighbours(field_in):
    padded = jnp.pad(field_in, ((0, 0), (1, 1), (1, 1), (1, 1)))
    return (padded[:, 2:, 1:-1, 1:-1], padded[:, :-2, 1:-1, 1:-1], padded[:, 1:-1, 2:, 1:-1], padded[:, 1:-1, :-2, 1:-1], padded[:, 1:-1, 1:-1, 2:], padded[:, 1:-1, 1:-1, :-2])

def reference(prior_heads, facies, facies_cond, well_cell, pump_rate, obs_test, obs_pair):
    conduct = facies_cond[facies]
    face_cond = [(conduct + neighbour[0]) * 0.5 for neighbour in neighbours(conduct[None])]
    diagonal = STORAGE + sum(face_cond)
    groups = TESTS // R_DEV
    cells = NX * NY * NZ

    def operate(field_in):
        result_field = diagonal * field_in
        for weight, neighbour in zip(face_cond, neighbours(field_in)):
            result_field = result_field - weight * neighbour
        return result_field

    def one_group(inputs):
        start_heads, wells, rates, first_local, second_local = inputs
        source = jnp.zeros((R_DEV, cells), start_heads.dtype)
        source = source.at[jnp.arange(R_DEV, dtype=jnp.int32), wells].set(-rates).reshape(start_heads.shape)
        head_field = start_heads
        residual = source - operate(start_heads)
        direction = residual
        norm_now = gram_local(residual, residual)
        for iteration in range(ITERS):
            applied = operate(direction)
            alpha_coef = solve_spd(gram_local(direction, applied), norm_now)
            head_field = head_field + combine(alpha_coef, direction)
            residual = residual - combine(alpha_coef, applied)
            if iteration + 1 < ITERS:
                norm_next = gram_local(residual, residual)
                beta_coef = solve_spd(norm_now, norm_next)
                direction = residual + combine(beta_coef, direction)
                norm_now = norm_next
        near_heads = neighbours(head_field)
        accumulated = jnp.zeros((OBS_DEV, NX, NY, NZ), jnp.float32)
        for direction_index in range(3):
            gradient = (near_heads[2 * direction_index] - near_heads[2 * direction_index + 1]) * 0.5
            accumulated = accumulated + jnp.take(gradient, first_local, axis=0) * jnp.take(gradient, second_local, axis=0)
        sensitivity = (-conduct * accumulated).astype(jnp.bfloat16).reshape(OBS_DEV, cells)
        return (head_field, sensitivity)
    offsets = (jnp.arange(groups, dtype=jnp.int32) * R_DEV)[:, None]
    first_all = (obs_test.reshape(groups, OBS_DEV) - offsets).astype(jnp.int32)
    second_all = (obs_pair.reshape(groups, OBS_DEV) - offsets).astype(jnp.int32)
    heads_out, sens_out = lax.map(one_group, (prior_heads.reshape(groups, R_DEV, NX, NY, NZ), well_cell.reshape(groups, R_DEV), pump_rate.reshape(groups, R_DEV), first_all, second_all))
    all_rows = sens_out.reshape(OBS, cells).astype(jnp.float32)
    jjt = jnp.dot(all_rows, all_rows.T, precision=HIGHEST_PRECISION) / float(cells)
    return (heads_out.reshape(TESTS, NX, NY, NZ), jjt)
```

```python
import functools

import jax
import jax.numpy as jnp
from jax import lax
from jax.experimental import pallas as pl
from jax.experimental.pallas import tpu as pltpu
from jax.sharding import PartitionSpec as P

STORAGE = 0.25
SCALE = 1.0 / 32.0
F32 = jnp.float32
BF16 = jnp.bfloat16
HIGHEST = lax.Precision.HIGHEST
CHUNKS = 4
PAD = 16
NT = (((1,), (1,)), ((), ()))
NN = (((1,), (0,)), ((), ()))


def split(value):
    high = value.astype(BF16)
    return high, (value - high.astype(F32)).astype(BF16)


def eliminate(table, first_lane, size):
    rows = lax.broadcasted_iota(jnp.int32, table.shape, 0)
    for k in range(size):
        lane = first_lane + k
        column = table[:, lane:lane + 1]
        pivot = table[k:k + 1, lane:lane + 1]
        scaled = table[k:k + 1, :] * (1.0 / pivot)
        table = jnp.where(rows == k, scaled, table - column * scaled)
    return table


def kernel(
    dims,
    prior, facies, facies_cond, well, rate, obs_test, obs_pair,
    heads, jjt,
    cond, cond_x, cond_y, cond_ys, weights,
    head_f, head_x, head_y,
    res_f, res_x, res_y,
    app_f, app_b, app_x, app_y, app_l,
    twice_f,
    res_h, res_l, res_xh, res_xl, res_yh, res_yl,
    fin_f, fin_x, fin_y,
    pick, sens, partial, part_y, part_x,
    sum_ax, sum_ay, sum_bx, sum_by,
    halo_send, halo_recv,
    ax_send, ax_recv, ay_send, ay_recv,
    rx_send, rx_recv, ry_send, ry_recv,
    ta_send, ta_recv,
):
    n_gx, n_gy, n_ta, group, rows_x, rows_y, layers, obs = dims
    gx, gy, ta = lax.axis_index("gx"), lax.axis_index("gy"), lax.axis_index("ta")
    cells = rows_x * rows_y
    size_y = rows_y * n_gy
    blocks = [(x, y) for x in range(rows_x) for y in range(rows_y)]
    owned = n_ta * obs // (n_gx * n_gy)
    owners = obs // owned
    padded = owners * PAD

    barrier = pltpu.get_barrier_semaphore()
    for axis, own, count in (("gx", gx, n_gx), ("gy", gy, n_gy), ("ta", ta, n_ta)):
        for step in range(1, count):
            pl.semaphore_signal(
                barrier, inc=1, device_id={axis: lax.rem(own + step, count)},
                device_id_type=pl.DeviceIdType.MESH,
            )

    def send(src, dst, send_sem, recv_sem, axis, peer):
        return pltpu.make_async_remote_copy(
            src_ref=src, dst_ref=dst, send_sem=send_sem, recv_sem=recv_sem,
            device_id={axis: peer}, device_id_type=pl.DeviceIdType.MESH,
        )

    up_x, down_x = lax.rem(gx + 1, n_gx), lax.rem(gx + n_gx - 1, n_gx)
    up_y, down_y = lax.rem(gy + 1, n_gy), lax.rem(gy + n_gy - 1, n_gy)
    lows = (gx > 0, gx < n_gx - 1, gy > 0, gy < n_gy - 1)
    outs = (gx < n_gx - 1, gx > 0, gy < n_gy - 1, gy > 0)

    def exchange(stage, sources, halo_x, halo_y):
        places = (halo_x.at[0], halo_x.at[1], halo_y.at[0], halo_y.at[1])
        axes = ("gx", "gx", "gy", "gy")
        peers = (up_x, down_x, up_y, down_y)
        return [
            send(src, dst, halo_send.at[stage, i], halo_recv.at[stage, i], axes[i], peers[i])
            for i, (src, dst) in enumerate(zip(sources, places))
        ]

    def start(copies):
        for copy, out in zip(copies, outs):
            pl.when(out)(copy.start)

    def arrived(copies):
        for copy, low in zip(copies, lows):
            pl.when(low)(copy.wait_recv)

    def sent(copies):
        for copy, out in zip(copies, outs):
            pl.when(out)(copy.wait_send)

    def faces(field):
        return (field.at[rows_x - 1], field.at[0], field.at[:, rows_y - 1], field.at[:, 0])

    kinds = facies[...]
    conduct = jnp.zeros(kinds.shape, F32)
    mean = jnp.float32(0.0)
    for c in range(facies_cond.shape[0]):
        conduct = jnp.where(kinds == c, facies_cond[c], conduct)
        mean = mean + facies_cond[c]
    cond[...] = conduct
    cond_ys[...] = jnp.zeros(cond_ys.shape, F32)
    for x in range(rows_x):
        cond_ys[0, x:x + 1, :] = conduct[(x + 1) * rows_y - 1:(x + 1) * rows_y]
        cond_ys[1, x:x + 1, :] = conduct[x * rows_y:x * rows_y + 1]
    shift = STORAGE + mean * (9.0 / facies_cond.shape[0])
    for x, y in blocks:
        head_f[x, y] = prior[pl.ds(x * rows_y + y, group, stride=cells), :]
    for side, low in enumerate(lows):
        @pl.when(jnp.logical_not(low))
        def _():
            for halo in ((cond_x, head_x, res_x, app_x) if side < 2 else (cond_y, head_y, res_y, app_y)):
                halo[side % 2] = jnp.zeros(halo.shape[1:], halo.dtype)

    pl.semaphore_wait(barrier, n_gx + n_gy + n_ta - 3)
    first_rows, last_rows = pl.ds(0, rows_y), pl.ds((rows_x - 1) * rows_y, rows_y)
    cond_copies = exchange(
        3, (cond.at[last_rows], cond.at[first_rows], cond_ys.at[0], cond_ys.at[1]), cond_x, cond_y
    )
    head_copies = exchange(0, faces(head_f), head_x, head_y)
    start(cond_copies)
    start(head_copies)

    lanes = lax.broadcasted_iota(jnp.int32, (group, layers), 1)
    tests = lax.broadcasted_iota(jnp.int32, (group, layers), 0)
    wells = jnp.zeros((group, layers), jnp.int32)
    rates = jnp.zeros((group, layers), F32)
    for t in range(group):
        wells = jnp.where(tests == t, well[t], wells)
        rates = jnp.where(tests == t, -rate[t], rates)
    wells = wells - lanes

    pad_rows = lax.broadcasted_iota(jnp.int32, (PAD, 128), 0)
    pad_lanes = lax.broadcasted_iota(jnp.int32, (PAD, 128), 1)
    slot = jnp.where(pad_lanes < 2 * group, lax.rem(pad_lanes, group), -2)
    for half, table in enumerate((obs_test, obs_pair)):
        for k in range(owners):
            named = jnp.full((PAD, 128), -1, jnp.int32)
            for j in range(owned):
                named = jnp.where(pad_rows == j, table[k * owned + j] - ta * group, named)
            pick[pl.ds(half * padded + k * PAD, PAD), :] = jnp.where(named == slot, 1.0, 0.0).astype(BF16)

    arrived(cond_copies)
    one_lane = lax.broadcasted_iota(jnp.int32, (1, layers), 1)
    for x, y in blocks:
        r = x * rows_y + y
        here = cond[r:r + 1, :]
        x_up = cond[r + rows_y:r + rows_y + 1, :] if x + 1 < rows_x else cond_x[1, y:y + 1, :]
        x_down = cond[r - rows_y:r - rows_y + 1, :] if x > 0 else cond_x[0, y:y + 1, :]
        y_up = cond[r + 1:r + 2, :] if y + 1 < rows_y else cond_y[1, x:x + 1, :]
        y_down = cond[r - 1:r, :] if y > 0 else cond_y[0, x:x + 1, :]
        z_up = jnp.where(one_lane < layers - 1, pltpu.roll(here, layers - 1, 1), 0.0)
        z_down = jnp.where(one_lane > 0, pltpu.roll(here, 1, 1), 0.0)
        face = [(here + other) * 0.5 for other in (x_up, x_down, y_up, y_down, z_up, z_down)]
        diagonal = STORAGE + sum(face)
        face[4] = jnp.where(one_lane < layers - 1, face[4], 0.0)
        face[5] = jnp.where(one_lane > 0, face[5], 0.0)
        for i, weight in enumerate(face):
            weights[i, r:r + 1, :] = weight
            weights[6 + i, r:r + 1, :] = weight * SCALE
        weights[12, r:r + 1, :] = diagonal
        weights[13, r:r + 1, :] = (diagonal - shift) * SCALE
        weights[14, r:r + 1, :] = diagonal * SCALE

    def weight(i, x, y):
        return weights[i, pl.ds(x * rows_y + y, 1), :]

    def inner(field, base, diag, x, y):
        here = field[x, y]
        total = weight(diag, x, y) * here
        if x + 1 < rows_x:
            total = total - weight(base, x, y) * field[x + 1, y]
        if x > 0:
            total = total - weight(base + 1, x, y) * field[x - 1, y]
        if y + 1 < rows_y:
            total = total - weight(base + 2, x, y) * field[x, y + 1]
        if y > 0:
            total = total - weight(base + 3, x, y) * field[x, y - 1]
        total = total - weight(base + 4, x, y) * pltpu.roll(here, layers - 1, 1)
        return total - weight(base + 5, x, y) * pltpu.roll(here, 1, 1)

    def outer(halo_x, halo_y, base, x, y):
        total = None
        terms = []
        if x == rows_x - 1:
            terms.append(weight(base, x, y) * halo_x[1, y].astype(F32))
        if x == 0:
            terms.append(weight(base + 1, x, y) * halo_x[0, y].astype(F32))
        if y == rows_y - 1:
            terms.append(weight(base + 2, x, y) * halo_y[1, x].astype(F32))
        if y == 0:
            terms.append(weight(base + 3, x, y) * halo_y[0, x].astype(F32))
        return sum(terms) if terms else None

    for x, y in blocks:
        cell = ((gx * rows_x + x) * size_y + gy * rows_y + y) * layers
        source = jnp.where(wells == cell, rates, 0.0)
        res_f[x, y] = source - inner(head_f, 0, 12, x, y)
    arrived(head_copies)
    for x, y in blocks:
        more = outer(head_x, head_y, 0, x, y)
        if more is not None:
            res_f[x, y] = res_f[x, y] + more
    res_copies = exchange(1, faces(res_f), res_x, res_y)
    start(res_copies)

    for x, y in blocks:
        app_f[x, y] = inner(res_f, 6, 13, x, y)
        res_h[x, y], res_l[x, y] = split(res_f[x, y])
    arrived(res_copies)
    for x, y in blocks:
        more = outer(res_x, res_y, 6, x, y)
        value = app_f[x, y]
        if more is not None:
            value = value - more
            app_f[x, y] = value
        app_b[x, y], app_l[x, y] = split(value)
    app_copies = exchange(2, faces(app_b), app_x, app_y)
    start(app_copies)

    stacked = jnp.concatenate(
        [
            jnp.concatenate([res_h[x, y], app_b[x, y], res_l[x, y], app_l[x, y]], axis=0)
            for x, y in blocks
        ],
        axis=1,
    )
    gram = lax.dot_general(stacked, stacked, NT, preferred_element_type=F32)
    gram = gram[:2 * group] + gram[2 * group:]
    gram = gram + pltpu.roll(gram, 2 * group, 1)
    table_lane = lax.broadcasted_iota(jnp.int32, (group, 4 * group), 1)

    def reduce_start(buffer, value, axis, own, count, sends, recvs):
        buffer[own] = value
        copies = []
        for step in range(1, count):
            peer = lax.rem(own + step, count)
            copies.append(send(buffer.at[own], buffer.at[own], sends.at[step], recvs.at[step], axis, peer))
            copies[-1].start()
        return copies

    def reduce_end(buffer, copies, count):
        for copy in copies:
            copy.wait_recv()
        total = buffer[0]
        for i in range(1, count):
            total = total + buffer[i]
        return total

    a_gx = reduce_start(
        sum_ax, jnp.where(table_lane < 2 * group, gram[:group], gram[group:]),
        "gx", gx, n_gx, ax_send.at[0], ax_recv.at[0],
    )
    for side in range(2):
        for y in range(rows_y):
            res_xh[side, y], res_xl[side, y] = split(res_x[side, y])
        for x in range(rows_x):
            res_yh[side, x], res_yl[side, x] = split(res_y[side, x])
    for x, y in blocks:
        twice_f[x, y] = inner(app_f, 6, 14, x, y)
    left = jnp.concatenate(
        [jnp.concatenate([app_b[x, y], app_l[x, y]], axis=0) for x, y in blocks], axis=1
    )
    arrived(app_copies)
    right = []
    for x, y in blocks:
        more = outer(app_x, app_y, 6, x, y)
        value = twice_f[x, y]
        high, low = split(value if more is None else value - more)
        right.append(jnp.concatenate([high, high, low, low], axis=0))
    gram = lax.dot_general(left, jnp.concatenate(right, axis=1), NT, preferred_element_type=F32)
    gram = gram[:group] + gram[group:]
    gram = gram + pltpu.roll(gram, 2 * group, 1)
    b_gx = reduce_start(sum_bx, gram, "gx", gx, n_gx, ax_send.at[1], ax_recv.at[1])
    total = reduce_end(sum_ax, a_gx, n_gx)
    a_gy = reduce_start(sum_ay, total, "gy", gy, n_gy, ay_send.at[0], ay_recv.at[0])
    total = reduce_end(sum_bx, b_gx, n_gx)
    b_gy = reduce_start(sum_by, total, "gy", gy, n_gy, ay_send.at[1], ay_recv.at[1])
    first = reduce_end(sum_ay, a_gy, n_gy)

    before = first + (shift * SCALE) * pltpu.roll(first, group, 1)
    before = jnp.where(table_lane < group, first, before)
    after = eliminate(before, group, group)
    keep = table_lane >= 3 * group
    gap = jnp.zeros((3 * group, 4 * group), F32)
    product = lax.dot_general(
        jnp.where(keep, before, 0.0), jnp.concatenate([gap, after], axis=0), NN,
        precision=HIGHEST, preferred_element_type=F32,
    )
    side = pltpu.roll(first, 3 * group, 1)
    second = reduce_end(sum_by, b_gy, n_gy)
    lower = eliminate(jnp.where(table_lane < group, side, second) - product, 3 * group, group)
    upper = after - lax.dot_general(
        jnp.where(keep, after, 0.0), jnp.concatenate([gap, lower], axis=0), NN,
        precision=HIGHEST, preferred_element_type=F32,
    )
    coef = jnp.concatenate([upper, lower, upper, lower], axis=0).T[:group] * SCALE
    coef_high, coef_low = split(coef)
    coef = jnp.concatenate([coef_high, coef_low], axis=0)

    def combined(bases, fields):
        right = jnp.concatenate([jnp.concatenate(parts, axis=0) for parts in fields], axis=1)
        change = lax.dot_general(coef, right, NN, preferred_element_type=F32)
        change = change[:group] + change[group:]
        return [base + change[:, i * layers:(i + 1) * layers] for i, base in enumerate(bases)]

    nothing = jnp.zeros((group, layers), BF16)
    work = []
    for x, y in blocks:
        work.append((fin_f, x, y, head_f, (res_h, app_b, res_l, app_l)))
    for s in range(2):
        for y in range(rows_y):
            work.append((fin_x, s, y, head_x, (res_xh, app_x, res_xl, None)))
        for x in range(rows_x):
            work.append((fin_y, s, x, head_y, (res_yh, app_y, res_yl, None)))
    for i in range(0, len(work), 2):
        pair = work[i:i + 2]
        results = combined(
            [base[a, b] for _, a, b, base, _ in pair],
            [[nothing if f is None else f[a, b] for f in parts] for _, a, b, _, parts in pair],
        )
        for (place, a, b, _, _), value in zip(pair, results):
            place[a, b] = value
            if place is fin_f:
                heads[pl.ds(a * rows_y + b, group, stride=cells), :] = value

    chosen = pick[:, :2 * group]
    per_chunk = cells // CHUNKS
    sens_copies = []
    for chunk in range(CHUNKS):
        for pos in range(0, per_chunk, 2):
            gradients = [[], [], []]
            conducts = []
            for x, y in blocks[chunk * per_chunk + pos:chunk * per_chunk + pos + 2]:
                here = fin_f[x, y]
                x_up = fin_f[x + 1, y] if x + 1 < rows_x else fin_x[1, y]
                x_down = fin_f[x - 1, y] if x > 0 else fin_x[0, y]
                y_up = fin_f[x, y + 1] if y + 1 < rows_y else fin_y[1, x]
                y_down = fin_f[x, y - 1] if y > 0 else fin_y[0, x]
                z_up = jnp.where(lanes < layers - 1, pltpu.roll(here, layers - 1, 1), 0.0)
                z_down = jnp.where(lanes > 0, pltpu.roll(here, 1, 1), 0.0)
                for d, (a, b) in enumerate(((x_up, x_down), (y_up, y_down), (z_up, z_down))):
                    gradients[d].append(jnp.concatenate(split((a - b) * 0.5), axis=0))
                r = x * rows_y + y
                conducts.append(cond[r:r + 1, :])
            total = None
            for d in range(3):
                taken = lax.dot_general(
                    chosen, jnp.concatenate(gradients[d], axis=1), NN, preferred_element_type=F32
                )
                term = taken[:padded] * taken[padded:]
                total = term if total is None else total + term
            value = (-jnp.concatenate(conducts, axis=1) * total).astype(BF16)
            sens[ta, chunk, :, pos * layers:(pos + 2) * layers] = value
        for step in range(1, n_ta):
            copy = send(
                sens.at[ta, chunk], sens.at[ta, chunk], ta_send.at[step, chunk],
                ta_recv.at[step, chunk], "ta", lax.rem(ta + step, n_ta),
            )
            copy.start()
            sens_copies.append((step, copy))

    def gathered(index):
        return jnp.concatenate([sens[index, chunk] for chunk in range(CHUNKS)], axis=1)

    for step in range(n_ta):
        for owner_step, copy in sens_copies:
            if owner_step == step:
                copy.wait_recv()
        index = lax.rem(ta + n_ta - step, n_ta)
        value = lax.dot_general(gathered(index), gathered(ta), NT, preferred_element_type=F32)
        for k in range(owners):
            b = index * owners + k
            partial[b // n_gy, lax.rem(b, n_gy)] = value[k * PAD:(k + 1) * PAD]

    y_copies = []
    for step in range(1, n_gy):
        peer = lax.rem(gy + step, n_gy)
        y_copies.append(
            send(partial.at[:, peer], part_y.at[step], ry_send.at[step], ry_recv.at[step], "gy", peer)
        )
        y_copies[-1].start()
    total = partial[:, gy]
    for i, copy in enumerate(y_copies):
        copy.wait_recv()
        total = total + part_y[i + 1]
    part_y[0] = total
    x_copies = []
    for step in range(1, n_gx):
        peer = lax.rem(gx + step, n_gx)
        x_copies.append(
            send(part_y.at[0, peer], part_x.at[step], rx_send.at[step], rx_recv.at[step], "gx", peer)
        )
        x_copies[-1].start()
    total = part_y[0, gx]
    for i, copy in enumerate(x_copies):
        copy.wait_recv()
        total = total + part_x[i + 1]
    out_rows = lax.broadcasted_iota(jnp.int32, (obs, padded), 0)
    out_lanes = lax.broadcasted_iota(jnp.int32, (obs, padded), 1)
    unpad = jnp.where((out_rows // owned) * PAD + lax.rem(out_rows, owned) == out_lanes, 1.0, 0.0)
    result = lax.dot_general(unpad, total, NT, precision=HIGHEST, preferred_element_type=F32)
    total_cells = rows_x * n_gx * size_y * layers
    jjt[...] = result[:, :owned] * (1.0 / float(total_cells))

    for copies in (cond_copies, head_copies, res_copies, app_copies):
        sent(copies)
    for copies in (a_gx, b_gx, a_gy, b_gy, y_copies, x_copies, [c for _, c in sens_copies]):
        for copy in copies:
            copy.wait_send()


def body(prior_heads, facies, facies_cond, well_cell, pump_rate, obs_test, obs_pair):
    n_gx, n_gy, n_ta = lax.axis_size("gx"), lax.axis_size("gy"), lax.axis_size("ta")
    group, rows_x, rows_y, layers = prior_heads.shape
    obs = obs_test.shape[0]
    cells = rows_x * rows_y
    owned = n_ta * obs // (n_gx * n_gy)
    padded = obs // owned * PAD
    own = (rows_x, rows_y, group, layers)
    at_x, at_y = (2, rows_y, group, layers), (2, rows_x, group, layers)
    f, b = (lambda shape: pltpu.VMEM(shape, F32)), (lambda shape: pltpu.VMEM(shape, BF16))
    wide = (group, 4 * group)
    sems = pltpu.SemaphoreType.DMA
    scratch = [
        f((cells, layers)), f((2, rows_y, layers)), f((2, 8, layers)), f((2, 8, layers)),
        f((15, cells, layers)),
        f(own), f(at_x), f(at_y),
        f(own), f(at_x), f(at_y),
        f(own), b(own), b(at_x), b(at_y), b(own),
        f(own),
        b(own), b(own), b(at_x), b(at_x), b(at_y), b(at_y),
        f(own), f(at_x), f(at_y),
        b((2 * padded, 128)), b((n_ta, CHUNKS, padded, cells // CHUNKS * layers)),
        f((n_gx, n_gy, PAD, padded)), f((n_gy, n_gx, PAD, padded)), f((n_gx, PAD, padded)),
        f((n_gx,) + wide), f((n_gy,) + wide), f((n_gx,) + wide), f((n_gy,) + wide),
        sems((4, 4)), sems((4, 4)),
        sems((2, n_gx)), sems((2, n_gx)), sems((2, n_gy)), sems((2, n_gy)),
        sems((n_gx,)), sems((n_gx,)), sems((n_gy,)), sems((n_gy,)),
        sems((n_ta, CHUNKS)), sems((n_ta, CHUNKS)),
    ]
    vmem, smem = pl.BlockSpec(memory_space=pltpu.VMEM), pl.BlockSpec(memory_space=pltpu.SMEM)
    heads, jjt = pl.pallas_call(
        functools.partial(kernel, (n_gx, n_gy, n_ta, group, rows_x, rows_y, layers, obs)),
        out_shape=(
            jax.ShapeDtypeStruct((group * cells, layers), F32),
            jax.ShapeDtypeStruct((obs, owned), F32),
        ),
        in_specs=[vmem, vmem, smem, smem, smem, smem, smem],
        out_specs=(vmem, vmem),
        scratch_shapes=scratch,
        compiler_params=pltpu.CompilerParams(
            collective_id=0, has_side_effects=True, vmem_limit_bytes=32 * 1024 * 1024
        ),
    )(
        prior_heads.reshape(group * cells, layers), facies.reshape(cells, layers),
        facies_cond, well_cell, pump_rate, obs_test, obs_pair,
    )
    return heads.reshape(prior_heads.shape), jjt


def solution(mesh):
    in_specs = (
        P("ta", "gx", "gy", None),
        P("gx", "gy", None),
        P(),
        P("ta"),
        P("ta"),
        P("ta"),
        P("ta"),
    )
    out_specs = (P("ta", "gx", "gy", None), P("ta", ("gx", "gy")))
    return jax.shard_map(body, mesh=mesh, in_specs=in_specs, out_specs=out_specs, check_vma=False)
```

```python
import functools

import jax
import jax.numpy as jnp
from jax import lax
from jax.experimental import pallas as pl
from jax.experimental.pallas import tpu as pltpu
from jax.sharding import PartitionSpec as P

STORAGE = 0.25
SCALE = 1.0 / 32.0
F32 = jnp.float32
BF16 = jnp.bfloat16
HIGHEST = lax.Precision.HIGHEST
CHUNKS = 4
PAD = 16
NT = (((1,), (1,)), ((), ()))
NN = (((1,), (0,)), ((), ()))


def split(value):
    high = value.astype(BF16)
    return high, (value - high.astype(F32)).astype(BF16)


def eliminate(table, first_lane, size):
    rows = lax.broadcasted_iota(jnp.int32, table.shape, 0)
    for k in range(size):
        lane = first_lane + k
        column = table[:, lane:lane + 1]
        pivot = table[k:k + 1, lane:lane + 1]
        scaled = table[k:k + 1, :] * (1.0 / pivot)
        table = jnp.where(rows == k, scaled, table - column * scaled)
    return table


def kernel(
    dims,
    prior, facies, facies_cond, well, rate, obs_test, obs_pair,
    heads, jjt,
    cond, cond_x, cond_y, cond_ys, weights,
    head_f, head_x, head_y,
    res_f, res_x, res_y,
    app_f, app_b, app_x, app_y, app_l,
    twice_f,
    res_h, res_l, res_xh, res_xl, res_yh, res_yl,
    fin_f, fin_x, fin_y,
    pick, sens, partial, parts,
    sum_ax, sum_ay, sum_b,
    halo_send, halo_recv,
    ax_send, ax_recv, ay_send, ay_recv,
    b_send, b_recv, p_send, p_recv,
    ta_send, ta_recv,
):
    n_gx, n_gy, n_ta, group, rows_x, rows_y, layers, obs = dims
    gx, gy, ta = lax.axis_index("gx"), lax.axis_index("gy"), lax.axis_index("ta")
    cells = rows_x * rows_y
    size_y = rows_y * n_gy
    blocks = [(x, y) for x in range(rows_x) for y in range(rows_y)]
    owned = n_ta * obs // (n_gx * n_gy)
    owners = obs // owned
    padded = owners * PAD

    barrier = pltpu.get_barrier_semaphore()
    tiles = n_gx * n_gy
    own_tile = gx * n_gy + gy
    steps = [(a, b) for a in range(n_gx) for b in range(n_gy) if a or b]
    others = [{"gx": lax.rem(gx + a, n_gx), "gy": lax.rem(gy + b, n_gy)} for a, b in steps]
    for peer in others + [{"ta": lax.rem(ta + step, n_ta)} for step in range(1, n_ta)]:
        pl.semaphore_signal(barrier, inc=1, device_id=peer, device_id_type=pl.DeviceIdType.MESH)

    def send(src, dst, send_sem, recv_sem, axis, peer):
        return send_to(src, dst, send_sem, recv_sem, {axis: peer})

    def send_to(src, dst, send_sem, recv_sem, device):
        return pltpu.make_async_remote_copy(
            src_ref=src, dst_ref=dst, send_sem=send_sem, recv_sem=recv_sem,
            device_id=device, device_id_type=pl.DeviceIdType.MESH,
        )

    up_x, down_x = lax.rem(gx + 1, n_gx), lax.rem(gx + n_gx - 1, n_gx)
    up_y, down_y = lax.rem(gy + 1, n_gy), lax.rem(gy + n_gy - 1, n_gy)
    lows = (gx > 0, gx < n_gx - 1, gy > 0, gy < n_gy - 1)
    outs = (gx < n_gx - 1, gx > 0, gy < n_gy - 1, gy > 0)

    def exchange(stage, sources, halo_x, halo_y):
        places = (halo_x.at[0], halo_x.at[1], halo_y.at[0], halo_y.at[1])
        axes = ("gx", "gx", "gy", "gy")
        peers = (up_x, down_x, up_y, down_y)
        return [
            send(src, dst, halo_send.at[stage, i], halo_recv.at[stage, i], axes[i], peers[i])
            for i, (src, dst) in enumerate(zip(sources, places))
        ]

    def start(copies):
        for copy, out in zip(copies, outs):
            pl.when(out)(copy.start)

    def arrived(copies):
        for copy, low in zip(copies, lows):
            pl.when(low)(copy.wait_recv)

    def sent(copies):
        for copy, out in zip(copies, outs):
            pl.when(out)(copy.wait_send)

    def faces(field):
        return (field.at[rows_x - 1], field.at[0], field.at[:, rows_y - 1], field.at[:, 0])

    kinds = facies[...]
    conduct = jnp.zeros(kinds.shape, F32)
    mean = jnp.float32(0.0)
    for c in range(facies_cond.shape[0]):
        conduct = jnp.where(kinds == c, facies_cond[c], conduct)
        mean = mean + facies_cond[c]
    cond[...] = conduct
    cond_ys[...] = jnp.zeros(cond_ys.shape, F32)
    for x in range(rows_x):
        cond_ys[0, x:x + 1, :] = conduct[(x + 1) * rows_y - 1:(x + 1) * rows_y]
        cond_ys[1, x:x + 1, :] = conduct[x * rows_y:x * rows_y + 1]
    shift = STORAGE + mean * (9.0 / facies_cond.shape[0])
    for x, y in blocks:
        head_f[x, y] = prior[pl.ds(x * rows_y + y, group, stride=cells), :]
    for side, low in enumerate(lows):
        @pl.when(jnp.logical_not(low))
        def _():
            for halo in ((cond_x, head_x, res_x, app_x) if side < 2 else (cond_y, head_y, res_y, app_y)):
                halo[side % 2] = jnp.zeros(halo.shape[1:], halo.dtype)

    pl.semaphore_wait(barrier, tiles + n_ta - 2)
    first_rows, last_rows = pl.ds(0, rows_y), pl.ds((rows_x - 1) * rows_y, rows_y)
    cond_copies = exchange(
        3, (cond.at[last_rows], cond.at[first_rows], cond_ys.at[0], cond_ys.at[1]), cond_x, cond_y
    )
    head_copies = exchange(0, faces(head_f), head_x, head_y)
    start(cond_copies)
    start(head_copies)

    lanes = lax.broadcasted_iota(jnp.int32, (group, layers), 1)
    tests = lax.broadcasted_iota(jnp.int32, (group, layers), 0)
    wells = jnp.zeros((group, layers), jnp.int32)
    rates = jnp.zeros((group, layers), F32)
    for t in range(group):
        wells = jnp.where(tests == t, well[t], wells)
        rates = jnp.where(tests == t, -rate[t], rates)
    wells = wells - lanes

    pad_rows = lax.broadcasted_iota(jnp.int32, (PAD, 128), 0)
    pad_lanes = lax.broadcasted_iota(jnp.int32, (PAD, 128), 1)
    slot = jnp.where(pad_lanes < 2 * group, lax.rem(pad_lanes, group), -2)
    for half, table in enumerate((obs_test, obs_pair)):
        for k in range(owners):
            named = jnp.full((PAD, 128), -1, jnp.int32)
            for j in range(owned):
                named = jnp.where(pad_rows == j, table[k * owned + j] - ta * group, named)
            pick[pl.ds(half * padded + k * PAD, PAD), :] = jnp.where(named == slot, 1.0, 0.0).astype(BF16)

    arrived(cond_copies)
    one_lane = lax.broadcasted_iota(jnp.int32, (1, layers), 1)
    for x, y in blocks:
        r = x * rows_y + y
        here = cond[r:r + 1, :]
        x_up = cond[r + rows_y:r + rows_y + 1, :] if x + 1 < rows_x else cond_x[1, y:y + 1, :]
        x_down = cond[r - rows_y:r - rows_y + 1, :] if x > 0 else cond_x[0, y:y + 1, :]
        y_up = cond[r + 1:r + 2, :] if y + 1 < rows_y else cond_y[1, x:x + 1, :]
        y_down = cond[r - 1:r, :] if y > 0 else cond_y[0, x:x + 1, :]
        z_up = jnp.where(one_lane < layers - 1, pltpu.roll(here, layers - 1, 1), 0.0)
        z_down = jnp.where(one_lane > 0, pltpu.roll(here, 1, 1), 0.0)
        face = [(here + other) * 0.5 for other in (x_up, x_down, y_up, y_down, z_up, z_down)]
        diagonal = STORAGE + sum(face)
        face[4] = jnp.where(one_lane < layers - 1, face[4], 0.0)
        face[5] = jnp.where(one_lane > 0, face[5], 0.0)
        for i, weight in enumerate(face):
            weights[i, r:r + 1, :] = weight
            weights[6 + i, r:r + 1, :] = weight * SCALE
        weights[12, r:r + 1, :] = diagonal
        weights[13, r:r + 1, :] = (diagonal - shift) * SCALE
        weights[14, r:r + 1, :] = diagonal * SCALE

    def weight(i, x, y):
        return weights[i, pl.ds(x * rows_y + y, 1), :]

    def inner(field, base, diag, x, y):
        here = field[x, y]
        total = weight(diag, x, y) * here
        if x + 1 < rows_x:
            total = total - weight(base, x, y) * field[x + 1, y]
        if x > 0:
            total = total - weight(base + 1, x, y) * field[x - 1, y]
        if y + 1 < rows_y:
            total = total - weight(base + 2, x, y) * field[x, y + 1]
        if y > 0:
            total = total - weight(base + 3, x, y) * field[x, y - 1]
        total = total - weight(base + 4, x, y) * pltpu.roll(here, layers - 1, 1)
        return total - weight(base + 5, x, y) * pltpu.roll(here, 1, 1)

    def outer(halo_x, halo_y, base, x, y):
        total = None
        terms = []
        if x == rows_x - 1:
            terms.append(weight(base, x, y) * halo_x[1, y].astype(F32))
        if x == 0:
            terms.append(weight(base + 1, x, y) * halo_x[0, y].astype(F32))
        if y == rows_y - 1:
            terms.append(weight(base + 2, x, y) * halo_y[1, x].astype(F32))
        if y == 0:
            terms.append(weight(base + 3, x, y) * halo_y[0, x].astype(F32))
        return sum(terms) if terms else None

    for x, y in blocks:
        cell = ((gx * rows_x + x) * size_y + gy * rows_y + y) * layers
        source = jnp.where(wells == cell, rates, 0.0)
        res_f[x, y] = source - inner(head_f, 0, 12, x, y)
    arrived(head_copies)
    for x, y in blocks:
        more = outer(head_x, head_y, 0, x, y)
        if more is not None:
            res_f[x, y] = res_f[x, y] + more
    res_copies = exchange(1, faces(res_f), res_x, res_y)
    start(res_copies)

    for x, y in blocks:
        app_f[x, y] = inner(res_f, 6, 13, x, y)
        res_h[x, y], res_l[x, y] = split(res_f[x, y])
    arrived(res_copies)
    for x, y in blocks:
        more = outer(res_x, res_y, 6, x, y)
        value = app_f[x, y]
        if more is not None:
            value = value - more
            app_f[x, y] = value
        app_b[x, y], app_l[x, y] = split(value)
    app_copies = exchange(2, faces(app_b), app_x, app_y)
    start(app_copies)

    stacked = jnp.concatenate(
        [
            jnp.concatenate([res_h[x, y], app_b[x, y], res_l[x, y], app_l[x, y]], axis=0)
            for x, y in blocks
        ],
        axis=1,
    )
    gram = lax.dot_general(stacked, stacked, NT, preferred_element_type=F32)
    gram = gram[:2 * group] + gram[2 * group:]
    gram = gram + pltpu.roll(gram, 2 * group, 1)
    table_lane = lax.broadcasted_iota(jnp.int32, (group, 4 * group), 1)

    def reduce_start(buffer, value, axis, own, count, sends, recvs):
        buffer[own] = value
        copies = []
        for step in range(1, count):
            peer = lax.rem(own + step, count)
            copies.append(send(buffer.at[own], buffer.at[own], sends.at[step], recvs.at[step], axis, peer))
            copies[-1].start()
        return copies

    def reduce_end(buffer, copies, count):
        for copy in copies:
            copy.wait_recv()
        total = buffer[0]
        for i in range(1, count):
            total = total + buffer[i]
        return total

    a_gx = reduce_start(
        sum_ax, jnp.where(table_lane < 2 * group, gram[:group], gram[group:]),
        "gx", gx, n_gx, ax_send, ax_recv,
    )
    for side in range(2):
        for y in range(rows_y):
            res_xh[side, y], res_xl[side, y] = split(res_x[side, y])
        for x in range(rows_x):
            res_yh[side, x], res_yl[side, x] = split(res_y[side, x])
    for x, y in blocks:
        twice_f[x, y] = inner(app_f, 6, 14, x, y)
    left = jnp.concatenate(
        [jnp.concatenate([app_b[x, y], app_l[x, y]], axis=0) for x, y in blocks], axis=1
    )
    arrived(app_copies)
    right = []
    for x, y in blocks:
        more = outer(app_x, app_y, 6, x, y)
        value = twice_f[x, y]
        high, low = split(value if more is None else value - more)
        right.append(jnp.concatenate([high, high, low, low], axis=0))
    gram = lax.dot_general(left, jnp.concatenate(right, axis=1), NT, preferred_element_type=F32)
    gram = gram[:group] + gram[group:]
    gram = gram + pltpu.roll(gram, 2 * group, 1)
    part = group // 4
    part_lane = lax.broadcasted_iota(jnp.int32, (part, 4 * group), 1)
    packed = gram[:part]
    for i in range(1, 4):
        packed = jnp.where(part_lane >= i * group, gram[i * part:(i + 1) * part], packed)
    sum_b[own_tile] = packed
    b_all = []
    for i, peer in enumerate(others):
        b_all.append(send_to(sum_b.at[own_tile], sum_b.at[own_tile], b_send.at[i], b_recv.at[i], peer))
        b_all[-1].start()
    total = reduce_end(sum_ax, a_gx, n_gx)
    a_gy = reduce_start(sum_ay, total, "gy", gy, n_gy, ay_send, ay_recv)
    first = reduce_end(sum_ay, a_gy, n_gy)

    before = first + (shift * SCALE) * pltpu.roll(first, group, 1)
    before = jnp.where(table_lane < group, first, before)
    after = eliminate(before, group, group)
    keep = table_lane >= 3 * group
    gap = jnp.zeros((3 * group, 4 * group), F32)
    product = lax.dot_general(
        jnp.where(keep, before, 0.0), jnp.concatenate([gap, after], axis=0), NN,
        precision=HIGHEST, preferred_element_type=F32,
    )
    side = pltpu.roll(first, 3 * group, 1)
    packed = reduce_end(sum_b, b_all, tiles)
    second = jnp.concatenate(
        [pltpu.roll(packed, (3 - i) * group, 1) if i < 3 else packed for i in range(4)], axis=0
    )
    lower = eliminate(jnp.where(table_lane < group, side, second) - product, 3 * group, group)
    upper = after - lax.dot_general(
        jnp.where(keep, after, 0.0), jnp.concatenate([gap, lower], axis=0), NN,
        precision=HIGHEST, preferred_element_type=F32,
    )
    coef = jnp.concatenate([upper, lower, upper, lower], axis=0).T[:group] * SCALE
    coef_high, coef_low = split(coef)
    coef = jnp.concatenate([coef_high, coef_low], axis=0)

    def combined(bases, fields):
        right = jnp.concatenate([jnp.concatenate(parts, axis=0) for parts in fields], axis=1)
        change = lax.dot_general(coef, right, NN, preferred_element_type=F32)
        change = change[:group] + change[group:]
        return [base + change[:, i * layers:(i + 1) * layers] for i, base in enumerate(bases)]

    nothing = jnp.zeros((group, layers), BF16)
    work = []
    for x, y in blocks:
        work.append((fin_f, x, y, head_f, (res_h, app_b, res_l, app_l)))
    for s in range(2):
        for y in range(rows_y):
            work.append((fin_x, s, y, head_x, (res_xh, app_x, res_xl, None)))
        for x in range(rows_x):
            work.append((fin_y, s, x, head_y, (res_yh, app_y, res_yl, None)))
    for i in range(0, len(work), 2):
        pair = work[i:i + 2]
        results = combined(
            [base[a, b] for _, a, b, base, _ in pair],
            [[nothing if f is None else f[a, b] for f in parts] for _, a, b, _, parts in pair],
        )
        for (place, a, b, _, _), value in zip(pair, results):
            place[a, b] = value
            if place is fin_f:
                heads[pl.ds(a * rows_y + b, group, stride=cells), :] = value

    chosen = pick[:, :2 * group]
    per_chunk = cells // CHUNKS
    sens_copies = []
    for chunk in range(CHUNKS):
        for pos in range(0, per_chunk, 2):
            gradients = [[], [], []]
            conducts = []
            for x, y in blocks[chunk * per_chunk + pos:chunk * per_chunk + pos + 2]:
                here = fin_f[x, y]
                x_up = fin_f[x + 1, y] if x + 1 < rows_x else fin_x[1, y]
                x_down = fin_f[x - 1, y] if x > 0 else fin_x[0, y]
                y_up = fin_f[x, y + 1] if y + 1 < rows_y else fin_y[1, x]
                y_down = fin_f[x, y - 1] if y > 0 else fin_y[0, x]
                z_up = jnp.where(lanes < layers - 1, pltpu.roll(here, layers - 1, 1), 0.0)
                z_down = jnp.where(lanes > 0, pltpu.roll(here, 1, 1), 0.0)
                for d, (a, b) in enumerate(((x_up, x_down), (y_up, y_down), (z_up, z_down))):
                    gradients[d].append(jnp.concatenate(split((a - b) * 0.5), axis=0))
                r = x * rows_y + y
                conducts.append(cond[r:r + 1, :])
            total = None
            for d in range(3):
                taken = lax.dot_general(
                    chosen, jnp.concatenate(gradients[d], axis=1), NN, preferred_element_type=F32
                )
                term = taken[:padded] * taken[padded:]
                total = term if total is None else total + term
            value = (-jnp.concatenate(conducts, axis=1) * total).astype(BF16)
            sens[ta, chunk, :, pos * layers:(pos + 2) * layers] = value
        for step in range(1, n_ta):
            copy = send(
                sens.at[ta, chunk], sens.at[ta, chunk], ta_send.at[step, chunk],
                ta_recv.at[step, chunk], "ta", lax.rem(ta + step, n_ta),
            )
            copy.start()
            sens_copies.append((step, copy))

    def gathered(index):
        return jnp.concatenate([sens[index, chunk] for chunk in range(CHUNKS)], axis=1)

    mine = gathered(ta)
    for step in range(n_ta):
        for owner_step, copy in sens_copies:
            if owner_step == step:
                copy.wait_recv()
        index = lax.rem(ta + n_ta - step, n_ta)
        value = lax.dot_general(
            mine if step == 0 else gathered(index), mine, NT, preferred_element_type=F32
        )
        for k in range(owners):
            b = index * owners + k
            partial[b] = value[k * PAD:k * PAD + owned]
            copy = send_to(
                partial.at[b], parts.at[own_tile], p_send.at[b], p_recv.at[own_tile],
                {"gx": b // n_gy, "gy": lax.rem(b, n_gy)},
            )
            pl.when(b != own_tile)(copy.start)
    total = partial[own_tile]
    part_copies = []
    for i, (a, b) in enumerate(steps):
        source = lax.rem(gx + n_gx - a, n_gx) * n_gy + lax.rem(gy + n_gy - b, n_gy)
        target = others[i]["gx"] * n_gy + others[i]["gy"]
        copy = send_to(partial.at[target], parts.at[source], p_send.at[target], p_recv.at[source], others[i])
        copy.wait_recv()
        part_copies.append(copy)
        total = total + parts[source]
    out_rows = lax.broadcasted_iota(jnp.int32, (obs, padded), 0)
    out_lanes = lax.broadcasted_iota(jnp.int32, (obs, padded), 1)
    unpad = jnp.where((out_rows // owned) * PAD + lax.rem(out_rows, owned) == out_lanes, 1.0, 0.0)
    result = lax.dot_general(total, unpad, NT, precision=HIGHEST, preferred_element_type=F32)
    total_cells = rows_x * n_gx * size_y * layers
    jjt[...] = result * (1.0 / float(total_cells))

    for copies in (cond_copies, head_copies, res_copies, app_copies):
        sent(copies)
    for copies in (a_gx, a_gy, b_all, part_copies, [c for _, c in sens_copies]):
        for copy in copies:
            copy.wait_send()


def body(prior_heads, facies, facies_cond, well_cell, pump_rate, obs_test, obs_pair):
    n_gx, n_gy, n_ta = lax.axis_size("gx"), lax.axis_size("gy"), lax.axis_size("ta")
    group, rows_x, rows_y, layers = prior_heads.shape
    obs = obs_test.shape[0]
    cells = rows_x * rows_y
    owned = n_ta * obs // (n_gx * n_gy)
    padded = obs // owned * PAD
    own = (rows_x, rows_y, group, layers)
    at_x, at_y = (2, rows_y, group, layers), (2, rows_x, group, layers)
    f, b = (lambda shape: pltpu.VMEM(shape, F32)), (lambda shape: pltpu.VMEM(shape, BF16))
    wide = (group, 4 * group)
    tiles = n_gx * n_gy
    sems = pltpu.SemaphoreType.DMA
    scratch = [
        f((cells, layers)), f((2, rows_y, layers)), f((2, 8, layers)), f((2, 8, layers)),
        f((15, cells, layers)),
        f(own), f(at_x), f(at_y),
        f(own), f(at_x), f(at_y),
        f(own), b(own), b(at_x), b(at_y), b(own),
        f(own),
        b(own), b(own), b(at_x), b(at_x), b(at_y), b(at_y),
        f(own), f(at_x), f(at_y),
        b((2 * padded, 128)), b((n_ta, CHUNKS, padded, cells // CHUNKS * layers)),
        f((tiles, owned, padded)), f((tiles, owned, padded)),
        f((n_gx,) + wide), f((n_gy,) + wide), f((tiles, group // 4, 4 * group)),
        sems((4, 4)), sems((4, 4)),
        sems((n_gx,)), sems((n_gx,)), sems((n_gy,)), sems((n_gy,)),
        sems((tiles,)), sems((tiles,)), sems((tiles,)), sems((tiles,)),
        sems((n_ta, CHUNKS)), sems((n_ta, CHUNKS)),
    ]
    vmem, smem = pl.BlockSpec(memory_space=pltpu.VMEM), pl.BlockSpec(memory_space=pltpu.SMEM)
    heads, jjt = pl.pallas_call(
        functools.partial(kernel, (n_gx, n_gy, n_ta, group, rows_x, rows_y, layers, obs)),
        out_shape=(
            jax.ShapeDtypeStruct((group * cells, layers), F32),
            jax.ShapeDtypeStruct((owned, obs), F32),
        ),
        in_specs=[vmem, vmem, smem, smem, smem, smem, smem],
        out_specs=(vmem, vmem),
        scratch_shapes=scratch,
        compiler_params=pltpu.CompilerParams(
            collective_id=0, has_side_effects=True, vmem_limit_bytes=32 * 1024 * 1024
        ),
    )(
        prior_heads.reshape(group * cells, layers), facies.reshape(cells, layers),
        facies_cond, well_cell, pump_rate, obs_test, obs_pair,
    )
    return heads.reshape(prior_heads.shape), jjt.T


def solution(mesh):
    in_specs = (
        P("ta", "gx", "gy", None),
        P("gx", "gy", None),
        P(),
        P("ta"),
        P("ta"),
        P("ta"),
        P("ta"),
    )
    out_specs = (P("ta", "gx", "gy", None), P("ta", ("gx", "gy")))
    return jax.shard_map(body, mesh=mesh, in_specs=in_specs, out_specs=out_specs, check_vma=False)
```

```python
import functools

import jax
import jax.numpy as jnp
from jax import lax
from jax.experimental import pallas as pl
from jax.experimental.pallas import tpu as pltpu
from jax.sharding import PartitionSpec as P

STORAGE = 0.25
SCALE = 1.0 / 32.0
F32 = jnp.float32
BF16 = jnp.bfloat16
HIGHEST = lax.Precision.HIGHEST
CHUNKS = 4
BLOCK = 4
PAD = 16
NT = (((1,), (1,)), ((), ()))
NN = (((1,), (0,)), ((), ()))


def split(value):
    high = value.astype(BF16)
    return high, (value - high.astype(F32)).astype(BF16)


def eliminate(table, first_lane, size):
    index = lax.broadcasted_iota(jnp.int32, table.shape, 0)
    for k in range(0, size, BLOCK):
        columns = [
            jnp.broadcast_to(table[:, first_lane + k + j:first_lane + k + j + 1], table.shape)
            for j in range(BLOCK)
        ]
        rows = [table[k + i:k + i + 1, :] for i in range(BLOCK)]
        corner = [[columns[j][k + i:k + i + 1, :] for j in range(BLOCK)] for i in range(BLOCK)]
        for i in range(BLOCK):
            inverse = 1.0 / corner[i][i]
            rows[i] = rows[i] * inverse
            for j in range(i + 1, BLOCK):
                corner[i][j] = corner[i][j] * inverse
            for m in range(BLOCK):
                if m != i:
                    rows[m] = rows[m] - corner[m][i] * rows[i]
                    for j in range(i + 1, BLOCK):
                        corner[m][j] = corner[m][j] - corner[m][i] * corner[i][j]
        for j in range(BLOCK):
            table = table - columns[j] * rows[j]
        for j in range(BLOCK):
            table = jnp.where(index == k + j, rows[j], table)
    return table


def kernel(
    dims,
    prior_in, facies_in, facies_cond, well, rate, obs_test, obs_pair,
    heads, jjt,
    cond, cond_x, cond_y, cond_ys, weights,
    head_f, head_x, head_y,
    res_f, res_x, res_y,
    app_f, app_b, app_x, app_y, app_l,
    twice_f,
    res_h, res_l, res_xh, res_xl, res_yh, res_yl,
    fin_f, fin_x, fin_y,
    pick, sens, partial, parts,
    sum_ax, sum_ay, sum_b,
    prior, facies, in_sem,
    halo_send, halo_recv,
    ax_send, ax_recv, ay_send, ay_recv,
    b_send, b_recv, p_send, p_recv,
    ta_send, ta_recv,
):
    n_gx, n_gy, n_ta, group, rows_x, rows_y, layers, obs = dims
    gx, gy, ta = lax.axis_index("gx"), lax.axis_index("gy"), lax.axis_index("ta")
    cells = rows_x * rows_y
    size_y = rows_y * n_gy
    blocks = [(x, y) for x in range(rows_x) for y in range(rows_y)]
    owned = n_ta * obs // (n_gx * n_gy)
    owners = obs // owned
    padded = owners * PAD

    loads = [
        pltpu.make_async_copy(facies_in, facies, in_sem.at[0]),
        pltpu.make_async_copy(prior_in, prior, in_sem.at[1]),
    ]
    for load in loads:
        load.start()
    barrier = pltpu.get_barrier_semaphore()
    tiles = n_gx * n_gy
    own_tile = gx * n_gy + gy
    steps = [(a, b) for a in range(n_gx) for b in range(n_gy) if a or b]
    others = [{"gx": lax.rem(gx + a, n_gx), "gy": lax.rem(gy + b, n_gy)} for a, b in steps]
    for peer in others + [{"ta": lax.rem(ta + step, n_ta)} for step in range(1, n_ta)]:
        pl.semaphore_signal(barrier, inc=1, device_id=peer, device_id_type=pl.DeviceIdType.MESH)

    def send(src, dst, send_sem, recv_sem, axis, peer):
        return send_to(src, dst, send_sem, recv_sem, {axis: peer})

    def send_to(src, dst, send_sem, recv_sem, device):
        return pltpu.make_async_remote_copy(
            src_ref=src, dst_ref=dst, send_sem=send_sem, recv_sem=recv_sem,
            device_id=device, device_id_type=pl.DeviceIdType.MESH,
        )

    up_x, down_x = lax.rem(gx + 1, n_gx), lax.rem(gx + n_gx - 1, n_gx)
    up_y, down_y = lax.rem(gy + 1, n_gy), lax.rem(gy + n_gy - 1, n_gy)
    lows = (gx > 0, gx < n_gx - 1, gy > 0, gy < n_gy - 1)
    outs = (gx < n_gx - 1, gx > 0, gy < n_gy - 1, gy > 0)

    def exchange(stage, sources, halo_x, halo_y):
        places = (halo_x.at[0], halo_x.at[1], halo_y.at[0], halo_y.at[1])
        axes = ("gx", "gx", "gy", "gy")
        peers = (up_x, down_x, up_y, down_y)
        return [
            send(src, dst, halo_send.at[stage, i], halo_recv.at[stage, i], axes[i], peers[i])
            for i, (src, dst) in enumerate(zip(sources, places))
        ]

    def start(copies):
        for copy, out in zip(copies, outs):
            pl.when(out)(copy.start)

    def arrived(copies):
        for copy, low in zip(copies, lows):
            pl.when(low)(copy.wait_recv)

    def sent(copies):
        for copy, out in zip(copies, outs):
            pl.when(out)(copy.wait_send)

    def faces(field):
        return (field.at[rows_x - 1], field.at[0], field.at[:, rows_y - 1], field.at[:, 0])

    loads[0].wait()
    kinds = facies[...]
    conduct = jnp.zeros(kinds.shape, F32)
    mean = jnp.float32(0.0)
    for c in range(facies_cond.shape[0]):
        conduct = jnp.where(kinds == c, facies_cond[c], conduct)
        mean = mean + facies_cond[c]
    cond[...] = conduct
    cond_ys[...] = jnp.zeros(cond_ys.shape, F32)
    for x in range(rows_x):
        cond_ys[0, x:x + 1, :] = conduct[(x + 1) * rows_y - 1:(x + 1) * rows_y]
        cond_ys[1, x:x + 1, :] = conduct[x * rows_y:x * rows_y + 1]
    shift = STORAGE + mean * (9.0 / facies_cond.shape[0])
    loads[1].wait()
    for x, y in blocks:
        head_f[x, y] = prior[pl.ds(x * rows_y + y, group, stride=cells), :]
    for side, low in enumerate(lows):
        @pl.when(jnp.logical_not(low))
        def _():
            for halo in ((cond_x, head_x, res_x, app_x) if side < 2 else (cond_y, head_y, res_y, app_y)):
                halo[side % 2] = jnp.zeros(halo.shape[1:], halo.dtype)

    pl.semaphore_wait(barrier, tiles + n_ta - 2)
    first_rows, last_rows = pl.ds(0, rows_y), pl.ds((rows_x - 1) * rows_y, rows_y)
    cond_copies = exchange(
        3, (cond.at[last_rows], cond.at[first_rows], cond_ys.at[0], cond_ys.at[1]), cond_x, cond_y
    )
    head_copies = exchange(0, faces(head_f), head_x, head_y)
    start(cond_copies)
    start(head_copies)

    lanes = lax.broadcasted_iota(jnp.int32, (group, layers), 1)
    tests = lax.broadcasted_iota(jnp.int32, (group, layers), 0)
    wells = jnp.zeros((group, layers), jnp.int32)
    rates = jnp.zeros((group, layers), F32)
    for t in range(group):
        wells = jnp.where(tests == t, well[t], wells)
        rates = jnp.where(tests == t, -rate[t], rates)
    wells = wells - lanes

    pad_rows = lax.broadcasted_iota(jnp.int32, (PAD, 128), 0)
    pad_lanes = lax.broadcasted_iota(jnp.int32, (PAD, 128), 1)
    slot = jnp.where(pad_lanes < 2 * group, lax.rem(pad_lanes, group), -2)
    for half, table in enumerate((obs_test, obs_pair)):
        for k in range(owners):
            named = jnp.full((PAD, 128), -1, jnp.int32)
            for j in range(owned):
                named = jnp.where(pad_rows == j, table[k * owned + j] - ta * group, named)
            pick[pl.ds(half * padded + k * PAD, PAD), :] = jnp.where(named == slot, 1.0, 0.0).astype(BF16)

    arrived(cond_copies)
    one_lane = lax.broadcasted_iota(jnp.int32, (1, layers), 1)
    for x, y in blocks:
        r = x * rows_y + y
        here = cond[r:r + 1, :]
        x_up = cond[r + rows_y:r + rows_y + 1, :] if x + 1 < rows_x else cond_x[1, y:y + 1, :]
        x_down = cond[r - rows_y:r - rows_y + 1, :] if x > 0 else cond_x[0, y:y + 1, :]
        y_up = cond[r + 1:r + 2, :] if y + 1 < rows_y else cond_y[1, x:x + 1, :]
        y_down = cond[r - 1:r, :] if y > 0 else cond_y[0, x:x + 1, :]
        z_up = jnp.where(one_lane < layers - 1, pltpu.roll(here, layers - 1, 1), 0.0)
        z_down = jnp.where(one_lane > 0, pltpu.roll(here, 1, 1), 0.0)
        face = [(here + other) * 0.5 for other in (x_up, x_down, y_up, y_down, z_up, z_down)]
        diagonal = STORAGE + sum(face)
        face[4] = jnp.where(one_lane < layers - 1, face[4], 0.0)
        face[5] = jnp.where(one_lane > 0, face[5], 0.0)
        for i, weight in enumerate(face):
            weights[i, r:r + 1, :] = weight
            weights[6 + i, r:r + 1, :] = weight * SCALE
        weights[12, r:r + 1, :] = diagonal
        weights[13, r:r + 1, :] = (diagonal - shift) * SCALE
        weights[14, r:r + 1, :] = diagonal * SCALE

    def weight(i, x, y):
        return weights[i, pl.ds(x * rows_y + y, 1), :]

    def inner(field, base, diag, x, y):
        here = field[x, y]
        total = weight(diag, x, y) * here
        if x + 1 < rows_x:
            total = total - weight(base, x, y) * field[x + 1, y]
        if x > 0:
            total = total - weight(base + 1, x, y) * field[x - 1, y]
        if y + 1 < rows_y:
            total = total - weight(base + 2, x, y) * field[x, y + 1]
        if y > 0:
            total = total - weight(base + 3, x, y) * field[x, y - 1]
        total = total - weight(base + 4, x, y) * pltpu.roll(here, layers - 1, 1)
        return total - weight(base + 5, x, y) * pltpu.roll(here, 1, 1)

    def outer(halo_x, halo_y, base, x, y):
        total = None
        terms = []
        if x == rows_x - 1:
            terms.append(weight(base, x, y) * halo_x[1, y].astype(F32))
        if x == 0:
            terms.append(weight(base + 1, x, y) * halo_x[0, y].astype(F32))
        if y == rows_y - 1:
            terms.append(weight(base + 2, x, y) * halo_y[1, x].astype(F32))
        if y == 0:
            terms.append(weight(base + 3, x, y) * halo_y[0, x].astype(F32))
        return sum(terms) if terms else None

    for x, y in blocks:
        cell = ((gx * rows_x + x) * size_y + gy * rows_y + y) * layers
        source = jnp.where(wells == cell, rates, 0.0)
        res_f[x, y] = source - inner(head_f, 0, 12, x, y)
    arrived(head_copies)
    for x, y in blocks:
        more = outer(head_x, head_y, 0, x, y)
        if more is not None:
            res_f[x, y] = res_f[x, y] + more
    res_copies = exchange(1, faces(res_f), res_x, res_y)
    start(res_copies)

    for x, y in blocks:
        app_f[x, y] = inner(res_f, 6, 13, x, y)
        res_h[x, y], res_l[x, y] = split(res_f[x, y])
    arrived(res_copies)
    for x, y in blocks:
        more = outer(res_x, res_y, 6, x, y)
        value = app_f[x, y]
        if more is not None:
            value = value - more
            app_f[x, y] = value
        app_b[x, y], app_l[x, y] = split(value)
    app_copies = exchange(2, faces(app_b), app_x, app_y)
    start(app_copies)

    stacked = jnp.concatenate(
        [
            jnp.concatenate([res_h[x, y], app_b[x, y], res_l[x, y], app_l[x, y]], axis=0)
            for x, y in blocks
        ],
        axis=1,
    )
    gram = lax.dot_general(stacked, stacked, NT, preferred_element_type=F32)
    gram = gram[:2 * group] + gram[2 * group:]
    gram = gram + pltpu.roll(gram, 2 * group, 1)
    table_lane = lax.broadcasted_iota(jnp.int32, (group, 4 * group), 1)

    def reduce_start(buffer, value, axis, own, count, sends, recvs):
        buffer[own] = value
        copies = []
        for step in range(1, count):
            peer = lax.rem(own + step, count)
            copies.append(send(buffer.at[own], buffer.at[own], sends.at[step], recvs.at[step], axis, peer))
            copies[-1].start()
        return copies

    def reduce_end(buffer, copies, count):
        for copy in copies:
            copy.wait_recv()
        total = buffer[0]
        for i in range(1, count):
            total = total + buffer[i]
        return total

    a_gx = reduce_start(
        sum_ax, jnp.where(table_lane < 2 * group, gram[:group], gram[group:]),
        "gx", gx, n_gx, ax_send, ax_recv,
    )
    for side in range(2):
        for y in range(rows_y):
            res_xh[side, y], res_xl[side, y] = split(res_x[side, y])
        for x in range(rows_x):
            res_yh[side, x], res_yl[side, x] = split(res_y[side, x])
    for x, y in blocks:
        twice_f[x, y] = inner(app_f, 6, 14, x, y)
    left = jnp.concatenate(
        [jnp.concatenate([app_b[x, y], app_l[x, y]], axis=0) for x, y in blocks], axis=1
    )
    total = reduce_end(sum_ax, a_gx, n_gx)
    a_gy = reduce_start(sum_ay, total, "gy", gy, n_gy, ay_send, ay_recv)
    arrived(app_copies)
    right = []
    for x, y in blocks:
        more = outer(app_x, app_y, 6, x, y)
        value = twice_f[x, y]
        high, low = split(value if more is None else value - more)
        right.append(jnp.concatenate([high, high, low, low], axis=0))
    gram = lax.dot_general(left, jnp.concatenate(right, axis=1), NT, preferred_element_type=F32)
    gram = gram[:group] + gram[group:]
    gram = gram + pltpu.roll(gram, 2 * group, 1)
    part = group // 4
    part_lane = lax.broadcasted_iota(jnp.int32, (part, 4 * group), 1)
    packed = gram[:part]
    for i in range(1, 4):
        packed = jnp.where(part_lane >= i * group, gram[i * part:(i + 1) * part], packed)
    sum_b[own_tile] = packed
    b_all = []
    for i, peer in enumerate(others):
        b_all.append(send_to(sum_b.at[own_tile], sum_b.at[own_tile], b_send.at[i], b_recv.at[i], peer))
        b_all[-1].start()
    first = reduce_end(sum_ay, a_gy, n_gy)

    before = first + (shift * SCALE) * pltpu.roll(first, group, 1)
    before = jnp.where(table_lane < group, first, before)
    after = eliminate(before, group, group)
    keep = table_lane >= 3 * group
    gap = jnp.zeros((3 * group, 4 * group), F32)
    product = lax.dot_general(
        jnp.where(keep, before, 0.0), jnp.concatenate([gap, after], axis=0), NN,
        precision=HIGHEST, preferred_element_type=F32,
    )
    side = pltpu.roll(first, 3 * group, 1)
    packed = reduce_end(sum_b, b_all, tiles)
    second = jnp.concatenate(
        [pltpu.roll(packed, (3 - i) * group, 1) if i < 3 else packed for i in range(4)], axis=0
    )
    lower = eliminate(jnp.where(table_lane < group, side, second) - product, 3 * group, group)
    upper = after - lax.dot_general(
        jnp.where(keep, after, 0.0), jnp.concatenate([gap, lower], axis=0), NN,
        precision=HIGHEST, preferred_element_type=F32,
    )
    coef = jnp.concatenate([upper, lower, upper, lower], axis=0).T[:group] * SCALE
    coef_high, coef_low = split(coef)
    coef = jnp.concatenate([coef_high, coef_low], axis=0)

    def combined(bases, fields):
        right = jnp.concatenate([jnp.concatenate(parts, axis=0) for parts in fields], axis=1)
        change = lax.dot_general(coef, right, NN, preferred_element_type=F32)
        change = change[:group] + change[group:]
        return [base + change[:, i * layers:(i + 1) * layers] for i, base in enumerate(bases)]

    nothing = jnp.zeros((group, layers), BF16)
    work = []
    for x, y in blocks:
        work.append((fin_f, x, y, head_f, (res_h, app_b, res_l, app_l)))
    for s in range(2):
        for y in range(rows_y):
            work.append((fin_x, s, y, head_x, (res_xh, app_x, res_xl, None)))
        for x in range(rows_x):
            work.append((fin_y, s, x, head_y, (res_yh, app_y, res_yl, None)))
    for i in range(0, len(work), 2):
        pair = work[i:i + 2]
        results = combined(
            [base[a, b] for _, a, b, base, _ in pair],
            [[nothing if f is None else f[a, b] for f in parts] for _, a, b, _, parts in pair],
        )
        for (place, a, b, _, _), value in zip(pair, results):
            place[a, b] = value
            if place is fin_f:
                heads[pl.ds(a * rows_y + b, group, stride=cells), :] = value

    chosen = pick[:, :2 * group]
    per_chunk = cells // CHUNKS
    sens_copies = []
    for chunk in range(CHUNKS):
        for pos in range(0, per_chunk, 2):
            gradients = [[], [], []]
            conducts = []
            for x, y in blocks[chunk * per_chunk + pos:chunk * per_chunk + pos + 2]:
                here = fin_f[x, y]
                x_up = fin_f[x + 1, y] if x + 1 < rows_x else fin_x[1, y]
                x_down = fin_f[x - 1, y] if x > 0 else fin_x[0, y]
                y_up = fin_f[x, y + 1] if y + 1 < rows_y else fin_y[1, x]
                y_down = fin_f[x, y - 1] if y > 0 else fin_y[0, x]
                z_up = jnp.where(lanes < layers - 1, pltpu.roll(here, layers - 1, 1), 0.0)
                z_down = jnp.where(lanes > 0, pltpu.roll(here, 1, 1), 0.0)
                for d, (a, b) in enumerate(((x_up, x_down), (y_up, y_down), (z_up, z_down))):
                    gradients[d].append(jnp.concatenate(split((a - b) * 0.5), axis=0))
                r = x * rows_y + y
                conducts.append(cond[r:r + 1, :])
            total = None
            for d in range(3):
                taken = lax.dot_general(
                    chosen, jnp.concatenate(gradients[d], axis=1), NN, preferred_element_type=F32
                )
                term = taken[:padded] * taken[padded:]
                total = term if total is None else total + term
            value = (-jnp.concatenate(conducts, axis=1) * total).astype(BF16)
            sens[ta, chunk, :, pos * layers:(pos + 2) * layers] = value
        for step in range(1, n_ta):
            copy = send(
                sens.at[ta, chunk], sens.at[ta, chunk], ta_send.at[step, chunk],
                ta_recv.at[step, chunk], "ta", lax.rem(ta + step, n_ta),
            )
            copy.start()
            sens_copies.append((step, copy))

    def gathered(index):
        return jnp.concatenate([sens[index, chunk] for chunk in range(CHUNKS)], axis=1)

    mine = gathered(ta)
    for step in range(n_ta):
        for owner_step, copy in sens_copies:
            if owner_step == step:
                copy.wait_recv()
        index = lax.rem(ta + n_ta - step, n_ta)
        value = lax.dot_general(
            mine if step == 0 else gathered(index), mine, NT, preferred_element_type=F32
        )
        for k in range(owners):
            b = index * owners + k
            partial[b] = value[k * PAD:k * PAD + owned]
            copy = send_to(
                partial.at[b], parts.at[own_tile], p_send.at[b], p_recv.at[own_tile],
                {"gx": b // n_gy, "gy": lax.rem(b, n_gy)},
            )
            pl.when(b != own_tile)(copy.start)
    total = partial[own_tile]
    part_copies = []
    for i, (a, b) in enumerate(steps):
        source = lax.rem(gx + n_gx - a, n_gx) * n_gy + lax.rem(gy + n_gy - b, n_gy)
        target = others[i]["gx"] * n_gy + others[i]["gy"]
        copy = send_to(partial.at[target], parts.at[source], p_send.at[target], p_recv.at[source], others[i])
        copy.wait_recv()
        part_copies.append(copy)
        total = total + parts[source]
    out_rows = lax.broadcasted_iota(jnp.int32, (obs, padded), 0)
    out_lanes = lax.broadcasted_iota(jnp.int32, (obs, padded), 1)
    unpad = jnp.where((out_rows // owned) * PAD + lax.rem(out_rows, owned) == out_lanes, 1.0, 0.0)
    result = lax.dot_general(total, unpad, NT, precision=HIGHEST, preferred_element_type=F32)
    total_cells = rows_x * n_gx * size_y * layers
    jjt[...] = result * (1.0 / float(total_cells))

    for copies in (cond_copies, head_copies, res_copies, app_copies):
        sent(copies)
    for copies in (a_gx, a_gy, b_all, part_copies, [c for _, c in sens_copies]):
        for copy in copies:
            copy.wait_send()


def body(prior_heads, facies, facies_cond, well_cell, pump_rate, obs_test, obs_pair):
    n_gx, n_gy, n_ta = lax.axis_size("gx"), lax.axis_size("gy"), lax.axis_size("ta")
    group, rows_x, rows_y, layers = prior_heads.shape
    obs = obs_test.shape[0]
    cells = rows_x * rows_y
    owned = n_ta * obs // (n_gx * n_gy)
    padded = obs // owned * PAD
    own = (rows_x, rows_y, group, layers)
    at_x, at_y = (2, rows_y, group, layers), (2, rows_x, group, layers)
    f, b = (lambda shape: pltpu.VMEM(shape, F32)), (lambda shape: pltpu.VMEM(shape, BF16))
    wide = (group, 4 * group)
    tiles = n_gx * n_gy
    sems = pltpu.SemaphoreType.DMA
    scratch = [
        f((cells, layers)), f((2, rows_y, layers)), f((2, 8, layers)), f((2, 8, layers)),
        f((15, cells, layers)),
        f(own), f(at_x), f(at_y),
        f(own), f(at_x), f(at_y),
        f(own), b(own), b(at_x), b(at_y), b(own),
        f(own),
        b(own), b(own), b(at_x), b(at_x), b(at_y), b(at_y),
        f(own), f(at_x), f(at_y),
        b((2 * padded, 128)), b((n_ta, CHUNKS, padded, cells // CHUNKS * layers)),
        f((tiles, owned, padded)), f((tiles, owned, padded)),
        f((n_gx,) + wide), f((n_gy,) + wide), f((tiles, group // 4, 4 * group)),
        f((group * cells, layers)), pltpu.VMEM((cells, layers), jnp.int32), sems((2,)),
        sems((4, 4)), sems((4, 4)),
        sems((n_gx,)), sems((n_gx,)), sems((n_gy,)), sems((n_gy,)),
        sems((tiles,)), sems((tiles,)), sems((tiles,)), sems((tiles,)),
        sems((n_ta, CHUNKS)), sems((n_ta, CHUNKS)),
    ]
    vmem, smem = pl.BlockSpec(memory_space=pltpu.VMEM), pl.BlockSpec(memory_space=pltpu.SMEM)
    anywhere = pl.BlockSpec(memory_space=pl.ANY)
    heads, jjt = pl.pallas_call(
        functools.partial(kernel, (n_gx, n_gy, n_ta, group, rows_x, rows_y, layers, obs)),
        out_shape=(
            jax.ShapeDtypeStruct((group * cells, layers), F32),
            jax.ShapeDtypeStruct((owned, obs), F32),
        ),
        in_specs=[anywhere, anywhere, smem, smem, smem, smem, smem],
        out_specs=(vmem, vmem),
        scratch_shapes=scratch,
        compiler_params=pltpu.CompilerParams(
            collective_id=0, has_side_effects=True, vmem_limit_bytes=56 * 1024 * 1024
        ),
    )(
        prior_heads.reshape(group * cells, layers), facies.reshape(cells, layers),
        facies_cond, well_cell, pump_rate, obs_test, obs_pair,
    )
    return heads.reshape(prior_heads.shape), jjt.T


def solution(mesh):
    in_specs = (
        P("ta", "gx", "gy", None),
        P("gx", "gy", None),
        P(),
        P("ta"),
        P("ta"),
        P("ta"),
        P("ta"),
    )
    out_specs = (P("ta", "gx", "gy", None), P("ta", ("gx", "gy")))
    return jax.shard_map(body, mesh=mesh, in_specs=in_specs, out_specs=out_specs, check_vma=False)
```
